32 devices in a mesh: tm: 2 (over core), space: 16 (over z, y, x).
Axes of the slice: x: 2, y: 2, z: 4, core: 2. Of those that a mesh axis runs over, the one named last changes fastest.
Arguments:
- increment_start: float32 [2, 8, 512, 1024], P('tm', None, 'space'), may hold values from -6 to 6
- dual_model_start: float32 [2, 8, 512, 1024], P('tm', None, 'space'), may hold values from -6 to 6
- dual_obs_start: bfloat16 [2, 256, 128], P('tm', 'space'), may hold values from -6 to 6
- model_rhs: float32 [2, 8, 512, 1024], P('tm', None, 'space'), may hold values from -6 to 6
- err_var: float32 [2, 8, 512, 1024], P('tm', None, 'space'), may hold values from 0.2 to 2
- decays: float32 [2, 8, 512, 1024], P('tm', None, 'space'), may hold values from 0.1 to 0.95
- scaling: float32 [8, 512, 1024], P(None, 'space'), may hold values from 0.5 to 1
- diffusion: float32 [8], replicated, may hold values from 0.05 to 0.24
- owners: int32 [2, 256], P('tm', 'space'), may hold values from 0 to 15, as said below
- tile_cols: int32 [2, 256, 128], P('tm', 'space'), may hold values from 0 to 32767, as said below
- jacobian: bfloat16 [2, 256, 128, 1024], P('tm', 'space'), may hold values from -0.1875 to 0.1875
- innovation: bfloat16 [2, 256, 128], P('tm', 'space'), may hold values from -6 to 6
- obs_var: bfloat16 [2, 256, 128], P('tm', 'space'), may hold values from 0.5 to 4
Outputs:
- dual_model: float32 [2, 8, 512, 1024], P('tm', None, 'space')
- dual_obs: float32 [2, 256, 128], P('tm', 'space')
- increment: float32 [2, 8, 512, 1024], P('tm', None, 'space')
The draws below stay inside these ranges and needn't reach their ends.
Inputs may be any that keep to these rules, and one draw needn't show every extreme that they name: `owners`: in each subwindow at most 2 of the 16 tiles of one device name the same owner, and one owner is named exactly 2 times by the tiles of every device. All 128 cells of a tile lie in one latitude row: tile_cols[k, t, c] // 1024 is the same for every c.
All inputs are finite; a program needn't handle non-finite values.
Results may differ from the reference program's by a relative error of at most 0.0042.
The reference program's roundings to bfloat16 on the way (of `gathered` and `tile_grad`) count: a program that leaves them out, or rounds other values in their place, can miss the bound.
Values may be sent and summed in bfloat16 or wider, within the bound.
A program may use at most 256 MiB of HBM per device.

```python
import math
import jax
import jax.numpy as jnp
from jax import lax

LEV = 8
TY = 32
LON = 1024
OBT_DEV = 16
OROWS = 128
TCOLS = 128
SUBSTEPS = 2
ITERS = 2
SUBWIN = 2
NY = 512
TILES = 256
CAP = 2
N_TM = 2
N_SPACE = 16


def draw_owners(key, part):
    pool_size = (N_SPACE - 1) * CAP
    hot_owner = jax.random.randint(jax.random.fold_in(key, 11), (N_TM, 1, 1), 0, N_SPACE)
    base_owner = jnp.arange(pool_size, dtype=jnp.int32) // CAP
    others = base_owner[None, None, :] + (base_owner[None, None, :] >= hot_owner).astype(jnp.int32)
    others = jnp.broadcast_to(others, (N_TM, N_SPACE, pool_size))
    scores = jax.random.randint(jax.random.fold_in(key, 12), (N_TM, N_SPACE, pool_size), 0, 2 ** 20) * pool_size
    scores = scores + jnp.arange(pool_size, dtype=jnp.int32)[None, None, :]
    order = jnp.argsort(scores, axis=-1)
    picked = jnp.take_along_axis(others, order, axis=-1)[:, :, :OBT_DEV - CAP]
    hot_rows = jnp.broadcast_to(hot_owner, (N_TM, N_SPACE, CAP))
    tiles_all = jnp.concatenate([hot_rows, picked], axis=-1)
    shuffle = jax.random.randint(jax.random.fold_in(key, 13), (N_TM, N_SPACE, OBT_DEV), 0, 2 ** 20) * OBT_DEV
    shuffle = shuffle + jnp.arange(OBT_DEV, dtype=jnp.int32)[None, None, :]
    placed = jnp.take_along_axis(tiles_all, jnp.argsort(shuffle, axis=-1), axis=-1)
    return placed.reshape(N_TM, N_SPACE * OBT_DEV).astype(jnp.int32)


def draw_tile_cols(key, part):
    row_pick = jax.random.randint(jax.random.fold_in(key, 21), (SUBWIN, TILES, 1), 0, TY)
    col_pick = jax.random.randint(jax.random.fold_in(key, 22), (SUBWIN, TILES, TCOLS), 0, LON)
    return (row_pick * LON + col_pick).astype(jnp.int32)


def shard_levels(key, dims, split, smallest, top_value):
    def one(position, shards_of):
        steps = jax.random.uniform(jax.random.fold_in(jax.random.fold_in(key, 6), position), (shards_of,), jnp.float32, smallest / len(split), top_value / len(split))
        return jnp.repeat(jnp.exp(steps), dims[position] // shards_of).reshape((-1,) + (1,) * (len(dims) - position - 1))

    loudness = one(*split[0])
    for cut in split[1:]:
        loudness = loudness * one(*cut)
    return loudness


def scatter_about(own_key, shape, deviation, most, pieces=(), kind=jnp.bfloat16):
    values = deviation * jax.random.normal(own_key, shape, jnp.float32)
    if pieces:
        values = values * shard_levels(own_key, shape, pieces, -0.22, 0.18)
    return jnp.clip(values, -most, most).astype(kind)


def setup_inputs(seed: int = 0) -> dict:
    keys = jax.random.split(jax.random.key(seed), 14)
    return {
        "increment_start": scatter_about(keys[0], (SUBWIN, LEV, NY, LON), 1.0, 6.0, ((0, 2), (2, 16)), jnp.float32),
        "dual_model_start": scatter_about(keys[1], (SUBWIN, LEV, NY, LON), 0.5, 6.0, ((0, 2), (2, 16)), jnp.float32),
        "dual_obs_start": scatter_about(keys[2], (SUBWIN, TILES, OROWS), 0.5, 6.0, ((0, 2), (1, 16))),
        "model_rhs": scatter_about(keys[3], (SUBWIN, LEV, NY, LON), 1.0, 6.0, ((0, 2), (2, 16)), jnp.float32),
        "err_var": jnp.clip(jnp.exp(math.log(2.0) - 2.3025851 * jax.random.uniform(keys[4], (SUBWIN, LEV, NY, LON), jnp.float32) ** shard_levels(keys[4], (SUBWIN, LEV, NY, LON), ((0, 2), (2, 16)), -0.2, 0.2)), 0.2, 2.0),
        "decays": jnp.clip(jnp.exp(math.log(0.95) - 2.2512918 * jax.random.uniform(keys[5], (SUBWIN, LEV, NY, LON), jnp.float32) ** shard_levels(keys[5], (SUBWIN, LEV, NY, LON), ((0, 2), (2, 16)), -0.2, 0.2)), 0.1, 0.95),
        "scaling": jnp.clip(jnp.exp(math.log(1.0) - 0.6931472 * jax.random.uniform(keys[6], (LEV, NY, LON), jnp.float32) ** shard_levels(keys[6], (LEV, NY, LON), ((1, 16),), -0.2, 0.2)), 0.5, 1.0),
        "diffusion": jnp.clip(jax.random.uniform(keys[7], (LEV,), jnp.float32, 0.05, 0.24), 0.05, 0.24),
        "owners": draw_owners(jax.random.fold_in(keys[13], 71), 0),
        "tile_cols": draw_tile_cols(jax.random.fold_in(keys[13], 71), 0),
        "jacobian": scatter_about(keys[10], (SUBWIN, TILES, OROWS, TCOLS * LEV), (TCOLS * LEV) ** -0.5, 0.1875, ((0, 2), (1, 16))),
        "innovation": scatter_about(keys[11], (SUBWIN, TILES, OROWS), 1.0, 6.0, ((0, 2), (1, 16))),
        "obs_var": jnp.clip(jnp.exp(math.log(4.0) - 2.0794415 * jax.random.uniform(keys[12], (SUBWIN, TILES, OROWS), jnp.float32) ** shard_levels(keys[12], (SUBWIN, TILES, OROWS), ((0, 2), (1, 16)), -0.2, 0.2)), 0.5, 4.0).astype(jnp.bfloat16),
    }


def model_apply(state_in, scaling, diffusion):
    current = state_in
    for repeat in range(SUBSTEPS):
        scaled = scaling * current
        padded = jnp.pad(scaled, ((0, 0), (1, 1), (0, 0)))
        laplace = padded[:, 2:] + padded[:, :-2] + jnp.roll(scaled, 1, 2) + jnp.roll(scaled, -1, 2) - 4.0 * scaled
        current = scaling * (scaled + diffusion[:, None, None] * laplace)
    return current


def window_model(fields, scaling, diffusion):
    return jax.vmap(model_apply, in_axes=(0, None, None))(fields, scaling, diffusion)


def gather_cells(fields, row_index, col_index):
    window_index = jnp.arange(SUBWIN, dtype=jnp.int32)[:, None, None]
    moved = jnp.transpose(fields, (0, 2, 3, 1))
    picked = moved[window_index, row_index, col_index]
    picked = picked.reshape(SUBWIN, TILES, TCOLS * LEV).astype(jnp.bfloat16)
    return lax.optimization_barrier(picked)


def obs_forward(jacobian, gathered):
    def per_window(operands):
        jac_rows, cells = operands
        return jnp.einsum("toj,tj->to", jac_rows.astype(jnp.float32), cells.astype(jnp.float32))
    return lax.map(per_window, (jacobian, gathered))


def obs_adjoint(jacobian, obs_dual, row_index, col_index):
    rounded = lax.optimization_barrier(obs_dual.astype(jnp.bfloat16))

    def per_window(operands):
        jac_rows, weights = operands
        summed = jnp.einsum("toj,to->tj", jac_rows.astype(jnp.float32), weights.astype(jnp.float32))
        return summed.astype(jnp.bfloat16)
    tile_grad = lax.optimization_barrier(lax.map(per_window, (jacobian, rounded)))
    window_index = jnp.arange(SUBWIN, dtype=jnp.int32)[:, None, None]
    values = tile_grad.astype(jnp.float32).reshape(SUBWIN, TILES, TCOLS, LEV)
    gridded = jnp.zeros((SUBWIN, NY, LON, LEV), jnp.float32).at[window_index, row_index, col_index].add(values)
    return jnp.transpose(gridded, (0, 3, 1, 2))


def reference(increment_start, dual_model_start, dual_obs_start, model_rhs, err_var, decays, scaling, diffusion, owners, tile_cols, jacobian, innovation, obs_var):
    row_index = (owners[:, :, None] * TY + tile_cols // LON).astype(jnp.int32)
    col_index = (tile_cols % LON).astype(jnp.int32)
    observed = innovation.astype(jnp.float32)
    obs_error = obs_var.astype(jnp.float32)
    increment = increment_start
    dual_model = dual_model_start
    obs_dual = dual_obs_start.astype(jnp.float32)
    zero_window = jnp.zeros_like(increment[:1])
    for repeat in range(ITERS):
        forward = jnp.concatenate([zero_window, window_model(increment[:-1], scaling, diffusion)], axis=0)
        backward = jnp.concatenate([window_model(dual_model[1:], scaling, diffusion), zero_window], axis=0)
        obs_image = obs_forward(jacobian, gather_cells(increment, row_index, col_index))
        adjoint_field = obs_adjoint(jacobian, obs_dual, row_index, col_index)
        r_model = model_rhs - err_var * dual_model - (increment - forward)
        r_obs = observed - obs_error * obs_dual - obs_image
        r_dual = -(dual_model - backward) - adjoint_field
        obs_dual = obs_dual + r_obs / obs_error
        carried = r_dual[SUBWIN - 1]
        upward_list = [carried]
        for window in range(SUBWIN - 2, -1, -1):
            carried = r_dual[window] + decays[window + 1] * carried
            upward_list.insert(0, carried)
        upward = jnp.stack(upward_list)
        dual_model = dual_model + upward
        source = r_model - err_var * upward
        carried = source[0]
        along_list = [carried]
        for window in range(1, SUBWIN):
            carried = source[window] + decays[window] * carried
            along_list.append(carried)
        increment = increment + jnp.stack(along_list)
    return dual_model, obs_dual, increment
```

```python
import functools

import jax
import jax.numpy as jnp
from jax import lax
from jax.experimental import pallas as pl
from jax.experimental.pallas import tpu as pltpu
from jax.sharding import PartitionSpec as P

SUBSTEPS = 2
ITERS = 2
EDGE = 8
F32 = jnp.float32
BF16 = jnp.bfloat16
MESH = pl.DeviceIdType.MESH
LOADS = ("inc", "dual", "rhs", "err", "dec", "scale", "field", "jac")


def contract(a, b, dims):
    return lax.dot_general(a, b, (dims, ((), ())), preferred_element_type=F32)


def kernel(
    n, cap,
    inc_in, dual_in, dobs_in, rhs_in, err_in, dec_in, scale_in, diff_ref, owners_ref,
    cols_ref, jac_in, innov_ref, ovar_ref,
    dual_out, dobs_out, inc_out,
    inc, dual, rhs, err, dec, scale, field, jac,
    adj, mfield, perm, perm_t, pick, pick_t, lines, packed, vmat, image, obs_dual,
    req_s, req_r, col_lo, col_hi, msg_s, msg_r, halo_s, halo_r, pair_s, pair_r,
    load_sem, out_sem, a2a_send, a2a_recv, halo_send, halo_recv, pair_send, pair_recv,
):
    me = lax.axis_index("space")
    tm = lax.axis_index("tm")
    lev, rows, width = inc.shape
    tiles, touched = cols_ref.shape[1:]
    slots = n * cap
    span = cap * lev
    groups = width // 128
    own = pl.ds(EDGE, rows)

    def load(k, src, dst):
        return pltpu.make_async_copy(src, dst, load_sem.at[LOADS.index(k)])

    loads = {
        "inc": load("inc", inc_in.at[0], inc),
        "dual": load("dual", dual_in.at[0], dual),
        "rhs": load("rhs", rhs_in.at[0], rhs),
        "err": load("err", err_in.at[0], err),
        "dec": load("dec", dec_in.at[0], dec),
        "scale": load("scale", scale_in, scale.at[:, own]),
        "jac": load("jac", jac_in.at[0], jac),
    }
    field_0 = load("field", inc_in.at[0], field.at[:, own])
    field_1 = load("field", dual_in.at[0], field.at[:, own])

    @pl.when(tm == 0)
    def _():
        field_0.start()

    @pl.when(tm == 1)
    def _():
        field_1.start()

    for name in ("scale", "jac", "inc", "dual", "dec", "rhs", "err"):
        loads[name].start()

    barrier = pltpu.get_barrier_semaphore()

    def greet(k, c):
        pl.semaphore_signal(
            barrier, inc=1, device_id={"space": lax.rem(me + k, n)}, device_id_type=MESH
        )
        return c

    lax.fori_loop(1, n, greet, 0)
    pl.semaphore_signal(barrier, inc=1, device_id={"tm": 1 - tm}, device_id_type=MESH)

    zero_rows = jnp.zeros((EDGE, width), F32)
    for l in range(lev):
        for ref in (field, scale):
            ref[l, pl.ds(0, EDGE), :] = zero_rows
            ref[l, pl.ds(EDGE + rows, EDGE), :] = zero_rows

    owner = [owners_ref[0, t] for t in range(tiles)]
    slot_of = []
    for t in range(tiles):
        rank = jnp.int32(0)
        for u in range(t):
            rank = rank + jnp.where(owner[u] == owner[t], 1, 0)
        slot_of.append(owner[t] * cap + rank)
    slot_row = lax.broadcasted_iota(jnp.int32, (slots, touched), 0)
    wide_row = lax.broadcasted_iota(jnp.int32, (slots * lev, touched), 0) // lev

    wanted = jnp.zeros((slots * lev, touched), jnp.int32)
    for t in range(tiles):
        wanted = jnp.where(wide_row == slot_of[t], cols_ref[0, pl.ds(t, 1), :], wanted)
    req_s[...] = wanted

    def block(i):
        return pl.ds(pl.multiple_of(i * span, span), span)

    def phase_refs(phase):
        if phase == 0:
            return req_s, req_r
        return msg_s.at[phase - 1], msg_r.at[phase - 1]

    def exchange(phase, to):
        src, dst = phase_refs(phase)
        return pltpu.make_async_remote_copy(
            src_ref=src.at[block(to)],
            dst_ref=dst.at[block(me)],
            send_sem=a2a_send.at[phase, to],
            recv_sem=a2a_recv.at[phase, me],
            device_id={"space": to},
            device_id_type=MESH,
        )

    def arrival(phase, frm):
        src, dst = phase_refs(phase)
        return pltpu.make_async_remote_copy(
            src_ref=src.at[block(frm)],
            dst_ref=dst.at[block(frm)],
            send_sem=a2a_send.at[phase, frm],
            recv_sem=a2a_recv.at[phase, frm],
            device_id={"space": frm},
            device_id_type=MESH,
        )

    def over_peers(act):
        def step(k, c):
            act(lax.rem(me + k, n))
            return c

        lax.fori_loop(1, n, step, 0)

    def send_all(phase):
        over_peers(lambda to: exchange(phase, to).start())
        src, dst = phase_refs(phase)
        dst[block(me), :] = src[block(me), :]

    def recv_all(phase):
        over_peers(lambda frm: arrival(phase, frm).wait_recv())

    pl.semaphore_wait(barrier, n)
    send_all(0)

    def halo_copy(it, way):
        count = 4 * lev if it == 0 else 2 * lev
        part = pl.ds(0, count)
        return pltpu.make_async_remote_copy(
            src_ref=halo_s.at[it, way, part],
            dst_ref=halo_r.at[it, way, part],
            send_sem=halo_send.at[it, way],
            recv_sem=halo_recv.at[it, way],
            device_id={"space": lax.rem(me + (n - 1 if way == 0 else 1), n)},
            device_id_type=MESH,
        )

    def halo_out(it):
        for way, first in ((0, EDGE), (1, EDGE + rows - 2)):
            for l in range(lev):
                halo_s[it, way, pl.ds(2 * l, 2), :] = field[l, pl.ds(first, 2), :]
                if it == 0:
                    halo_s[it, way, pl.ds(2 * (lev + l), 2), :] = scale[l, pl.ds(first, 2), :]

        @pl.when(me > 0)
        def _():
            halo_copy(it, 0).start()

        @pl.when(me < n - 1)
        def _():
            halo_copy(it, 1).start()

    def halo_in(it):
        def place(way, first):
            halo_copy(it, way).wait_recv()
            for l in range(lev):
                field[l, pl.ds(first, 2), :] = halo_r[it, way, pl.ds(2 * l, 2), :]
                if it == 0:
                    scale[l, pl.ds(first, 2), :] = halo_r[it, way, pl.ds(2 * (lev + l), 2), :]

        @pl.when(me < n - 1)
        def _():
            place(0, EDGE + rows)

        @pl.when(me > 0)
        def _():
            place(1, EDGE - 2)

    def pair_copy(it, kind, l):
        return pltpu.make_async_remote_copy(
            src_ref=pair_s.at[it, kind, l],
            dst_ref=pair_r.at[it, kind, l],
            send_sem=pair_send.at[it, kind, l],
            recv_sem=pair_recv.at[it, kind, l],
            device_id={"tm": 1 - tm},
            device_id_type=MESH,
        )

    def per_level(act):
        def step(l, c):
            act(l)
            return c

        lax.fori_loop(0, lev, step, 0)

    def model(l):
        factor = scale[l]
        current = field[l]
        tall = current.shape[0]
        for repeat in range(SUBSTEPS):
            scaled = factor * current
            laplace = (
                pltpu.roll(scaled, 1, 0)
                + pltpu.roll(scaled, tall - 1, 0)
                + pltpu.roll(scaled, 1, 1)
                + pltpu.roll(scaled, width - 1, 1)
                - 4.0 * scaled
            )
            current = factor * (scaled + diff_ref[l] * laplace)
        return current[EDGE : EDGE + rows]

    def adjoint_out(phase):
        rounded = obs_dual[...].astype(BF16).astype(F32)
        for t in range(tiles):
            row = jnp.where(slot_row == slot_of[t], rounded[t : t + 1, :], 0.0)
            vmat[:, pl.ds(t * touched, touched)] = row.astype(BF16)
        flat = jac[...].reshape(tiles * jac.shape[1], jac.shape[2])
        grad = contract(vmat[...], flat, ((1,), (0,))).astype(BF16)
        grad = contract(grad, perm_t[...], ((1,), (0,)))
        for l in range(lev):
            packed[pl.ds(l, slots, stride=lev), :] = grad[:, l * touched : (l + 1) * touched]
        phase_refs(phase)[0][...] = packed[...].astype(BF16)
        send_all(phase)

    def columns_out(phase):
        flat = inc[...].reshape(lev * rows, width).astype(BF16)
        lines[...] = contract(pick[...], flat, ((1,), (0,)))
        found = jnp.zeros((slots * lev, touched), F32)
        for h in range(groups):
            part = jnp.take_along_axis(
                lines[:, h * 128 : (h + 1) * 128], col_lo[...], axis=1, mode="promise_in_bounds"
            )
            found = jnp.where(col_hi[...] == h, part, found)
        phase_refs(phase)[0][...] = found.astype(BF16)
        send_all(phase)

    def observe(phase):
        recv_all(phase)
        packed[...] = phase_refs(phase)[1][...].astype(F32)
        cells = jnp.concatenate(
            [packed[pl.ds(l, slots, stride=lev), :] for l in range(lev)], axis=1
        ).astype(BF16)
        cells = contract(cells, perm[...], ((1,), (0,))).astype(BF16)
        flat = jac[...].reshape(tiles * jac.shape[1], jac.shape[2])
        seen = contract(cells, flat, ((1,), (1,)))
        for t in range(tiles):
            mine = jnp.where(slot_row == slot_of[t], seen[:, t * touched : (t + 1) * touched], 0.0)
            image[pl.ds(t, 1), :] = jnp.sum(mine, axis=0, keepdims=True)
        variance = ovar_ref[0].astype(F32)
        held = obs_dual[...]
        residual = innov_ref[0].astype(F32) - variance * held - image[...]
        obs_dual[...] = held + residual / variance

    def spread(phase):
        recv_all(phase)
        packed[...] = phase_refs(phase)[1][...].astype(F32)
        lane_row = lax.broadcasted_iota(jnp.int32, (128, touched), 0)

        def slot_lines(s, c):
            here = pl.ds(pl.multiple_of(s * lev, lev), lev)
            values, high, low = packed[here, :], col_hi[here, :], col_lo[here, :]
            left = jnp.concatenate(
                [jnp.where(high == h, values, 0.0) for h in range(groups)], axis=0
            ).astype(BF16)
            places = jnp.concatenate([low] * (128 // lev), axis=0)
            onehot = jnp.where(places == lane_row, 1.0, 0.0).astype(BF16)
            line = contract(left, onehot, ((1,), (1,)))
            for h in range(groups):
                lines[here, pl.ds(h * 128, 128)] = line[h * lev : (h + 1) * lev]
            return c

        def four(s, c):
            for u in range(4):
                slot_lines(4 * s + u, c)
            return c

        lax.fori_loop(0, slots // 4, four, 0)
        whole = lines[...]
        high = whole.astype(BF16)
        low = (whole - high.astype(F32)).astype(BF16)
        total = contract(pick_t[...], high, ((1,), (0,))) + contract(
            pick_t[...], low, ((1,), (0,))
        )
        adj[...] = total.reshape(lev, rows, width)

    loads["scale"].wait()
    field_0.wait()
    halo_out(0)

    cells_all = touched * lev
    first = lax.broadcasted_iota(jnp.int32, (cells_all, cells_all), 0)
    second = lax.broadcasted_iota(jnp.int32, (cells_all, cells_all), 1)
    perm_t[...] = jnp.where((first % lev) * touched + first // lev == second, 1.0, 0.0).astype(BF16)
    perm[...] = jnp.where((first % touched) * lev + first // touched == second, 1.0, 0.0).astype(
        BF16
    )
    obs_dual[...] = dobs_in[0].astype(F32)
    loads["jac"].wait()
    adjoint_out(1)

    recv_all(0)
    cell = req_r[...]
    column = cell % width
    col_lo[...] = column % 128
    col_hi[...] = column // 128
    line_of = cell // width
    level_of = lax.broadcasted_iota(jnp.int32, (slots * lev, touched), 0) % lev
    place = level_of * rows + line_of
    lane = lax.broadcasted_iota(jnp.int32, (slots * lev, touched), 1)
    chosen = jnp.concatenate(
        [
            jnp.where(place == lane + first_lane, 1.0, 0.0)
            for first_lane in range(0, lev * rows, touched)
        ],
        axis=1,
    )
    pick[...] = chosen.astype(BF16)
    pick_t[...] = chosen.T.astype(BF16)

    loads["inc"].wait()
    columns_out(2)
    loads["dual"].wait()
    loads["dec"].wait()
    loads["rhs"].wait()
    loads["err"].wait()

    for it in range(ITERS):
        last = it == ITERS - 1
        grad_phase, cols_phase = 1 + 2 * it, 2 + 2 * it
        halo_in(it)

        @pl.when(tm == 0)
        def _():
            def go(l):
                pair_s[it, 0, l] = model(l)
                pair_copy(it, 0, l).start()

            per_level(go)

        @pl.when(tm == 1)
        def _():
            def go(l):
                mfield[l] = model(l)

            per_level(go)

        spread(grad_phase)

        @pl.when(tm == 1)
        def _():
            def go(l):
                upward = -dual[l] - adj[l]
                pair_s[it, 2, l] = mfield[l] + dec[l] * upward
                pair_copy(it, 2, l).start()
                r_model = rhs[l] - err[l] * dual[l] - inc[l]
                mfield[l] = r_model - err[l] * upward
                raised = dual[l] + upward
                dual[l] = raised
                if not last:
                    field[l, own, :] = raised
                else:
                    pltpu.make_async_copy(dual.at[l], dual_out.at[0, l], out_sem.at[0, l]).start()

            per_level(go)

        if not last:
            observe(cols_phase)
            adjoint_out(grad_phase + 2)

        @pl.when(tm == 0)
        def _():
            def go(l):
                pair_copy(it, 2, l).wait_recv()
                upward = pair_r[it, 2, l] - dual[l] - adj[l]
                along = rhs[l] - err[l] * dual[l] - inc[l] - err[l] * upward
                pair_s[it, 1, l] = along
                pair_copy(it, 1, l).start()
                dual[l] = dual[l] + upward
                moved = inc[l] + along
                inc[l] = moved
                if not last:
                    field[l, own, :] = moved
                else:
                    pltpu.make_async_copy(dual.at[l], dual_out.at[0, l], out_sem.at[0, l]).start()
                    pltpu.make_async_copy(inc.at[l], inc_out.at[0, l], out_sem.at[1, l]).start()

            per_level(go)

        if not last:
            halo_out(it + 1)
        else:
            observe(cols_phase)
            dobs_out[0] = obs_dual[...]

        @pl.when(tm == 1)
        def _():
            def go(l):
                pair_copy(it, 0, l).wait_recv()
                pair_copy(it, 1, l).wait_recv()
                along = mfield[l] + pair_r[it, 0, l] + dec[l] * pair_r[it, 1, l]
                inc[l] = inc[l] + along
                if last:
                    pltpu.make_async_copy(inc.at[l], inc_out.at[0, l], out_sem.at[1, l]).start()

            per_level(go)

        if not last:
            columns_out(cols_phase + 2)

    for phase in range(1 + 2 * ITERS):
        over_peers(lambda to: exchange(phase, to).wait_send())
    for it in range(ITERS):

        @pl.when(me > 0)
        def _():
            halo_copy(it, 0).wait_send()

        @pl.when(me < n - 1)
        def _():
            halo_copy(it, 1).wait_send()

        @pl.when(tm == 0)
        def _():
            per_level(lambda l: pair_copy(it, 0, l).wait_send())
            per_level(lambda l: pair_copy(it, 1, l).wait_send())

        @pl.when(tm == 1)
        def _():
            per_level(lambda l: pair_copy(it, 2, l).wait_send())

    per_level(lambda l: pltpu.make_async_copy(dual.at[l], dual_out.at[0, l], out_sem.at[0, l]).wait())
    per_level(lambda l: pltpu.make_async_copy(inc.at[l], inc_out.at[0, l], out_sem.at[1, l]).wait())


def on_device(*args):
    increment_start, jacobian, tile_cols = args[0], args[10], args[9]
    lev, rows, width = increment_start.shape[1:]
    tiles, touched = tile_cols.shape[1:]
    orows = jacobian.shape[2]
    n = lax.axis_size("space")
    cap = max(2, 2 * tiles // n)
    slots = n * cap
    cells = touched * lev
    grid = (lev, rows, width)
    tall = (lev, rows + 2 * EDGE, width)
    hbm = pl.BlockSpec(memory_space=pl.ANY)
    vmem = pl.BlockSpec(memory_space=pltpu.VMEM)
    smem = pl.BlockSpec(memory_space=pltpu.SMEM)
    dma = pltpu.SemaphoreType.DMA
    scratch = [
        pltpu.VMEM(grid, F32),
        pltpu.VMEM(grid, F32),
        pltpu.VMEM(grid, F32),
        pltpu.VMEM(grid, F32),
        pltpu.VMEM(grid, F32),
        pltpu.VMEM(tall, F32),
        pltpu.VMEM(tall, F32),
        pltpu.VMEM((tiles, orows, cells), BF16),
        pltpu.VMEM(grid, F32),
        pltpu.VMEM(grid, F32),
        pltpu.VMEM((cells, cells), BF16),
        pltpu.VMEM((cells, cells), BF16),
        pltpu.VMEM((slots * lev, lev * rows), BF16),
        pltpu.VMEM((lev * rows, slots * lev), BF16),
        pltpu.VMEM((slots * lev, width), F32),
        pltpu.VMEM((slots * lev, touched), F32),
        pltpu.VMEM((slots, tiles * orows), BF16),
        pltpu.VMEM((tiles, orows), F32),
        pltpu.VMEM((tiles, orows), F32),
        pltpu.VMEM((slots * lev, touched), jnp.int32),
        pltpu.VMEM((slots * lev, touched), jnp.int32),
        pltpu.VMEM((slots * lev, touched), jnp.int32),
        pltpu.VMEM((slots * lev, touched), jnp.int32),
        pltpu.VMEM((2 * ITERS, slots * lev, touched), BF16),
        pltpu.VMEM((2 * ITERS, slots * lev, touched), BF16),
        pltpu.VMEM((ITERS, 2, 4 * lev, width), F32),
        pltpu.VMEM((ITERS, 2, 4 * lev, width), F32),
        pltpu.VMEM((ITERS, 3) + grid, F32),
        pltpu.VMEM((ITERS, 3) + grid, F32),
        dma((len(LOADS),)),
        dma((2, lev)),
        dma((1 + 2 * ITERS, n)),
        dma((1 + 2 * ITERS, n)),
        dma((ITERS, 2)),
        dma((ITERS, 2)),
        dma((ITERS, 3, lev)),
        dma((ITERS, 3, lev)),
    ]
    return pl.pallas_call(
        functools.partial(kernel, n, cap),
        out_shape=(
            jax.ShapeDtypeStruct((1,) + grid, F32),
            jax.ShapeDtypeStruct((1, tiles, orows), F32),
            jax.ShapeDtypeStruct((1,) + grid, F32),
        ),
        in_specs=[hbm, hbm, vmem, hbm, hbm, hbm, hbm, smem, smem, vmem, hbm, vmem, vmem],
        out_specs=(hbm, vmem, hbm),
        scratch_shapes=scratch,
        compiler_params=pltpu.CompilerParams(
            collective_id=0, has_side_effects=True, vmem_limit_bytes=60 * 2**20
        ),
        name="assimilate",
    )(*args)


def solution(mesh):
    in_specs = (
        P("tm", None, "space", None),
        P("tm", None, "space", None),
        P("tm", "space", None),
        P("tm", None, "space", None),
        P("tm", None, "space", None),
        P("tm", None, "space", None),
        P(None, "space", None),
        P(),
        P("tm", "space"),
        P("tm", "space", None),
        P("tm", "space", None, None),
        P("tm", "space", None),
        P("tm", "space", None),
    )
    out_specs = (P("tm", None, "space", None), P("tm", "space", None), P("tm", None, "space", None))
    return jax.shard_map(
        on_device, mesh=mesh, in_specs=in_specs, out_specs=out_specs, check_vma=False
    )
```

```python
import functools

import jax
import jax.numpy as jnp
from jax import lax
from jax.experimental import pallas as pl
from jax.experimental.pallas import tpu as pltpu
from jax.sharding import PartitionSpec as P

SUBSTEPS = 2
ITERS = 2
EDGE = 8
F32 = jnp.float32
BF16 = jnp.bfloat16
MESH = pl.DeviceIdType.MESH
LOADS = ("inc", "dual", "rhs", "err", "dec", "scale", "field", "jac")


def shift_of(size):
    assert size & (size - 1) == 0
    return size.bit_length() - 1


def reorder(cells, parts, dtype):
    row = lax.broadcasted_iota(jnp.int32, (cells, 128), 0)
    lane = lax.broadcasted_iota(jnp.int32, (cells, 128), 1)
    target = (row & (parts - 1)) * (cells // parts) + (row >> shift_of(parts)) - lane
    return jnp.concatenate(
        [jnp.where(target == at, 1.0, 0.0).astype(dtype) for at in range(0, cells, 128)], axis=1
    )


def contract(a, b, dims):
    return lax.dot_general(a, b, (dims, ((), ())), preferred_element_type=F32)


def kernel(
    n, cap,
    inc_in, dual_in, dobs_in, rhs_in, err_in, dec_in, scale_in, diff_ref, owners_ref,
    cols_ref, jac_in, innov_ref, ovar_ref,
    dual_out, dobs_out, inc_out,
    inc, dual, rhs, err, dec, scale, field, jac,
    adj, mfield, source, perm, perm_t, pick, pick_t, lines, packed, vmat, image, obs_dual,
    req_s, req_r, col_lo, col_hi, msg_s, msg_r, halo_s, halo_r, pair_s, pair_r,
    load_sem, out_sem, a2a_send, a2a_recv, halo_send, halo_recv, pair_send, pair_recv,
):
    me = lax.axis_index("space")
    tm = lax.axis_index("tm")
    lev, rows, width = inc.shape
    tiles, touched = cols_ref.shape[1:]
    slots = n * cap
    span = cap * lev
    groups = width // 128
    own = pl.ds(EDGE, rows)

    def load(k, src, dst):
        return pltpu.make_async_copy(src, dst, load_sem.at[LOADS.index(k)])

    loads = {
        "inc": load("inc", inc_in.at[0], inc),
        "dual": load("dual", dual_in.at[0], dual),
        "rhs": load("rhs", rhs_in.at[0], rhs),
        "err": load("err", err_in.at[0], err),
        "dec": load("dec", dec_in.at[0], dec),
        "scale": load("scale", scale_in, scale.at[:, own]),
        "jac": load("jac", jac_in.at[0], jac),
    }
    field_0 = load("field", inc_in.at[0], field.at[:, own])
    field_1 = load("field", dual_in.at[0], field.at[:, own])

    @pl.when(tm == 0)
    def _():
        field_0.start()

    @pl.when(tm == 1)
    def _():
        field_1.start()

    for name in ("scale", "jac", "inc", "dual", "dec", "rhs", "err"):
        loads[name].start()

    barrier = pltpu.get_barrier_semaphore()

    def greet(k, c):
        pl.semaphore_signal(
            barrier, inc=1, device_id={"space": lax.rem(me + k, n)}, device_id_type=MESH
        )
        return c

    lax.fori_loop(1, n, greet, 0)
    pl.semaphore_signal(barrier, inc=1, device_id={"tm": 1 - tm}, device_id_type=MESH)

    zero_rows = jnp.zeros((EDGE, width), F32)
    for l in range(lev):
        for ref in (field, scale):
            ref[l, pl.ds(0, EDGE), :] = zero_rows
            ref[l, pl.ds(EDGE + rows, EDGE), :] = zero_rows

    owner = [owners_ref[0, t] for t in range(tiles)]
    slot_of = []
    for t in range(tiles):
        rank = jnp.int32(0)
        for u in range(t):
            rank = rank + jnp.where(owner[u] == owner[t], 1, 0)
        slot_of.append(owner[t] * cap + rank)
    slot_row = lax.broadcasted_iota(jnp.int32, (slots, touched), 0)
    wide_row = lax.broadcasted_iota(jnp.int32, (slots * lev, touched), 0) >> shift_of(lev)

    wanted = jnp.zeros((slots * lev, touched), jnp.int32)
    for t in range(tiles):
        wanted = jnp.where(wide_row == slot_of[t], cols_ref[0, pl.ds(t, 1), :], wanted)
    req_s[...] = wanted

    def block(i):
        return pl.ds(pl.multiple_of(i * span, span), span)

    def phase_refs(phase):
        if phase == 0:
            return req_s, req_r
        return msg_s.at[phase - 1], msg_r.at[phase - 1]

    def exchange(phase, to):
        src, dst = phase_refs(phase)
        return pltpu.make_async_remote_copy(
            src_ref=src.at[block(to)],
            dst_ref=dst.at[block(me)],
            send_sem=a2a_send.at[phase, to],
            recv_sem=a2a_recv.at[phase, me],
            device_id={"space": to},
            device_id_type=MESH,
        )

    def arrival(phase, frm):
        src, dst = phase_refs(phase)
        return pltpu.make_async_remote_copy(
            src_ref=src.at[block(frm)],
            dst_ref=dst.at[block(frm)],
            send_sem=a2a_send.at[phase, frm],
            recv_sem=a2a_recv.at[phase, frm],
            device_id={"space": frm},
            device_id_type=MESH,
        )

    def over_peers(act):
        def step(k, c):
            act(lax.rem(me + k, n))
            return c

        lax.fori_loop(1, n, step, 0)

    def send_all(phase):
        over_peers(lambda to: exchange(phase, to).start())
        src, dst = phase_refs(phase)
        dst[block(me), :] = src[block(me), :]

    def recv_all(phase):
        over_peers(lambda frm: arrival(phase, frm).wait_recv())

    pl.semaphore_wait(barrier, n)
    send_all(0)

    def halo_copy(it, way):
        count = 4 * lev if it == 0 else 2 * lev
        part = pl.ds(0, count)
        return pltpu.make_async_remote_copy(
            src_ref=halo_s.at[it, way, part],
            dst_ref=halo_r.at[it, way, part],
            send_sem=halo_send.at[it, way],
            recv_sem=halo_recv.at[it, way],
            device_id={"space": lax.rem(me + (n - 1 if way == 0 else 1), n)},
            device_id_type=MESH,
        )

    def halo_out(it):
        for way, first in ((0, EDGE), (1, EDGE + rows - 2)):
            for l in range(lev):
                halo_s[it, way, pl.ds(2 * l, 2), :] = field[l, pl.ds(first, 2), :]
                if it == 0:
                    halo_s[it, way, pl.ds(2 * (lev + l), 2), :] = scale[l, pl.ds(first, 2), :]

        @pl.when(me > 0)
        def _():
            halo_copy(it, 0).start()

        @pl.when(me < n - 1)
        def _():
            halo_copy(it, 1).start()

    def halo_in(it):
        def place(way, first):
            halo_copy(it, way).wait_recv()
            for l in range(lev):
                field[l, pl.ds(first, 2), :] = halo_r[it, way, pl.ds(2 * l, 2), :]
                if it == 0:
                    scale[l, pl.ds(first, 2), :] = halo_r[it, way, pl.ds(2 * (lev + l), 2), :]

        @pl.when(me < n - 1)
        def _():
            place(0, EDGE + rows)

        @pl.when(me > 0)
        def _():
            place(1, EDGE - 2)

    def pair_copy(it, kind, l):
        return pltpu.make_async_remote_copy(
            src_ref=pair_s.at[it, kind, l],
            dst_ref=pair_r.at[it, kind, l],
            send_sem=pair_send.at[it, kind, l],
            recv_sem=pair_recv.at[it, kind, l],
            device_id={"tm": 1 - tm},
            device_id_type=MESH,
        )

    def per_level(act):
        def step(l, c):
            act(l)
            return c

        lax.fori_loop(0, lev, step, 0)

    def model(l):
        factor = scale[l]
        current = field[l]
        tall = current.shape[0]
        for repeat in range(SUBSTEPS):
            scaled = factor * current
            laplace = (
                pltpu.roll(scaled, 1, 0)
                + pltpu.roll(scaled, tall - 1, 0)
                + pltpu.roll(scaled, 1, 1)
                + pltpu.roll(scaled, width - 1, 1)
                - 4.0 * scaled
            )
            current = factor * (scaled + diff_ref[l] * laplace)
        return current[EDGE : EDGE + rows]

    def adjoint_out(phase):
        rounded = obs_dual[...].astype(BF16).astype(F32)
        for t in range(tiles):
            row = jnp.where(slot_row == slot_of[t], rounded[t : t + 1, :], 0.0)
            vmat[:, pl.ds(t * touched, touched)] = row.astype(BF16)
        flat = jac[...].reshape(tiles * jac.shape[1], jac.shape[2])
        grad = contract(vmat[...], flat, ((1,), (0,))).astype(BF16)
        grad = contract(grad, perm_t[...], ((1,), (0,)))
        for l in range(lev):
            packed[pl.ds(l, slots, stride=lev), :] = grad[:, l * touched : (l + 1) * touched]
        phase_refs(phase)[0][...] = packed[...].astype(BF16)
        send_all(phase)

    def columns_out(phase):
        flat = inc[...].reshape(lev * rows, width).astype(BF16)
        lines[...] = contract(pick[...], flat, ((1,), (0,)))
        found = jnp.zeros((slots * lev, touched), F32)
        for h in range(groups):
            part = jnp.take_along_axis(
                lines[:, h * 128 : (h + 1) * 128], col_lo[...], axis=1, mode="promise_in_bounds"
            )
            found = jnp.where(col_hi[...] == h, part, found)
        phase_refs(phase)[0][...] = found.astype(BF16)
        send_all(phase)

    def observe(phase):
        recv_all(phase)
        packed[...] = phase_refs(phase)[1][...].astype(F32)
        cells = jnp.concatenate(
            [packed[pl.ds(l, slots, stride=lev), :] for l in range(lev)], axis=1
        ).astype(BF16)
        cells = contract(cells, perm[...], ((1,), (0,))).astype(BF16)
        flat = jac[...].reshape(tiles * jac.shape[1], jac.shape[2])
        seen = contract(cells, flat, ((1,), (1,)))
        for t in range(tiles):
            mine = jnp.where(slot_row == slot_of[t], seen[:, t * touched : (t + 1) * touched], 0.0)
            image[pl.ds(t, 1), :] = jnp.sum(mine, axis=0, keepdims=True)
        variance = ovar_ref[0].astype(F32)
        held = obs_dual[...]
        residual = innov_ref[0].astype(F32) - variance * held - image[...]
        obs_dual[...] = held + residual / variance

    def spread(phase):
        recv_all(phase)
        packed[...] = phase_refs(phase)[1][...].astype(F32)
        lane_row = lax.broadcasted_iota(jnp.int32, (128, touched), 0)

        def slot_lines(s, c):
            here = pl.ds(pl.multiple_of(s * lev, lev), lev)
            values, high, low = packed[here, :], col_hi[here, :], col_lo[here, :]
            left = jnp.concatenate(
                [jnp.where(high == h, values, 0.0) for h in range(groups)], axis=0
            ).astype(BF16)
            places = jnp.concatenate([low] * (128 // lev), axis=0)
            onehot = jnp.where(places == lane_row, 1.0, 0.0).astype(BF16)
            line = contract(left, onehot, ((1,), (1,)))
            for h in range(groups):
                lines[here, pl.ds(h * 128, 128)] = line[h * lev : (h + 1) * lev]
            return c

        def eight(s, c):
            for u in range(8):
                slot_lines(8 * s + u, c)
            return c

        lax.fori_loop(0, slots // 8, eight, 0)
        whole = lines[...]
        high = whole.astype(BF16)
        low = (whole - high.astype(F32)).astype(BF16)
        total = contract(pick_t[...], high, ((1,), (0,))) + contract(
            pick_t[...], low, ((1,), (0,))
        )
        adj[...] = total.reshape(lev, rows, width)

    loads["scale"].wait()
    field_0.wait()
    halo_out(0)

    cells_all = touched * lev
    perm_t[...] = reorder(cells_all, lev, BF16)
    perm[...] = reorder(cells_all, touched, BF16)
    obs_dual[...] = dobs_in[0].astype(F32)
    loads["jac"].wait()
    adjoint_out(1)

    recv_all(0)
    cell = req_r[...]
    col_lo[...] = cell & 127
    col_hi[...] = (cell & (width - 1)) >> 7
    line_of = cell >> shift_of(width)
    level_of = lax.broadcasted_iota(jnp.int32, (slots * lev, touched), 0) & (lev - 1)
    place = level_of * rows + line_of
    lane = lax.broadcasted_iota(jnp.int32, (slots * lev, touched), 1)
    chosen = jnp.concatenate(
        [
            jnp.where(place == lane + first_lane, 1.0, 0.0)
            for first_lane in range(0, lev * rows, touched)
        ],
        axis=1,
    )
    pick[...] = chosen.astype(BF16)
    pick_t[...] = chosen.T.astype(BF16)

    loads["inc"].wait()
    columns_out(2)
    loads["dual"].wait()
    loads["dec"].wait()
    loads["rhs"].wait()
    loads["err"].wait()

    def forward_model(it):
        halo_in(it)

        def go(l):
            pair_s[it, 0, l] = model(l)
            pair_copy(it, 0, l).start()

        per_level(go)

    def backward_model(it):
        halo_in(it)

        def go(l):
            mfield[l] = model(l)

        per_level(go)

    def write_out(l, which):
        held, out = ((dual, dual_out), (inc, inc_out))[which]
        return pltpu.make_async_copy(held.at[l], out.at[0, l], out_sem.at[which, l])

    for it in range(ITERS):
        last = it == ITERS - 1
        grad_phase, cols_phase = 1 + 2 * it, 2 + 2 * it
        if it == 0:

            @pl.when(tm == 0)
            def _():
                forward_model(it)

            @pl.when(tm == 1)
            def _():
                backward_model(it)

        spread(grad_phase)

        @pl.when(tm == 1)
        def _():
            def go(l):
                upward = -dual[l] - adj[l]
                pair_s[it, 2, l] = mfield[l] + dec[l] * upward
                pair_copy(it, 2, l).start()
                r_model = rhs[l] - err[l] * dual[l] - inc[l]
                source[l] = r_model - err[l] * upward
                raised = dual[l] + upward
                dual[l] = raised
                if not last:
                    field[l, own, :] = raised
                else:
                    write_out(l, 0).start()

            per_level(go)
            if not last:
                halo_out(it + 1)

        if not last:
            observe(cols_phase)
            adjoint_out(grad_phase + 2)

        @pl.when(tm == 0)
        def _():
            if it > 0:
                forward_model(it)

            def go(l):
                pair_copy(it, 2, l).wait_recv()
                upward = pair_r[it, 2, l] - dual[l] - adj[l]
                along = rhs[l] - err[l] * dual[l] - inc[l] - err[l] * upward
                pair_s[it, 1, l] = along
                pair_copy(it, 1, l).start()
                dual[l] = dual[l] + upward
                moved = inc[l] + along
                inc[l] = moved
                if not last:
                    field[l, own, :] = moved
                else:
                    write_out(l, 0).start()
                    write_out(l, 1).start()

            per_level(go)
            if not last:
                halo_out(it + 1)

        if last:
            observe(cols_phase)
            dobs_out[0] = obs_dual[...]

        @pl.when(tm == 1)
        def _():
            if not last:
                backward_model(it + 1)

            def go(l):
                pair_copy(it, 0, l).wait_recv()
                pair_copy(it, 1, l).wait_recv()
                along = source[l] + pair_r[it, 0, l] + dec[l] * pair_r[it, 1, l]
                inc[l] = inc[l] + along
                if last:
                    write_out(l, 1).start()

            per_level(go)

        if not last:
            columns_out(cols_phase + 2)

    for phase in range(1 + 2 * ITERS):
        over_peers(lambda to: exchange(phase, to).wait_send())
    for it in range(ITERS):

        @pl.when(me > 0)
        def _():
            halo_copy(it, 0).wait_send()

        @pl.when(me < n - 1)
        def _():
            halo_copy(it, 1).wait_send()

        @pl.when(tm == 0)
        def _():
            per_level(lambda l: pair_copy(it, 0, l).wait_send())
            per_level(lambda l: pair_copy(it, 1, l).wait_send())

        @pl.when(tm == 1)
        def _():
            per_level(lambda l: pair_copy(it, 2, l).wait_send())

    per_level(lambda l: write_out(l, 0).wait())
    per_level(lambda l: write_out(l, 1).wait())


def deliver(*refs):
    count = (len(refs) - 1) // 2
    sources, targets, sem = refs[:count], refs[count : 2 * count], refs[-1]
    copies = []
    for src, dst in zip(sources, targets):
        for part in range(sem.shape[1]) if src.shape[1] == sem.shape[1] else (None,):
            here = slice(None) if part is None else pl.ds(part, 1)
            copies.append(
                pltpu.make_async_copy(
                    src.at[:, here], dst.at[:, here], sem.at[len(copies) // sem.shape[1], part or 0]
                )
            )
    for copy in copies:
        copy.start()
    for copy in copies:
        copy.wait()


def on_device(*args):
    increment_start, jacobian, tile_cols = args[0], args[10], args[9]
    lev, rows, width = increment_start.shape[1:]
    tiles, touched = tile_cols.shape[1:]
    orows = jacobian.shape[2]
    n = lax.axis_size("space")
    cap = max(2, 2 * tiles // n)
    slots = n * cap
    cells = touched * lev
    grid = (lev, rows, width)
    tall = (lev, rows + 2 * EDGE, width)
    hbm = pl.BlockSpec(memory_space=pl.ANY)
    vmem = pl.BlockSpec(memory_space=pltpu.VMEM)
    smem = pl.BlockSpec(memory_space=pltpu.SMEM)
    dma = pltpu.SemaphoreType.DMA
    scratch = [
        pltpu.VMEM(grid, F32),
        pltpu.VMEM(grid, F32),
        pltpu.VMEM(grid, F32),
        pltpu.VMEM(grid, F32),
        pltpu.VMEM(grid, F32),
        pltpu.VMEM(tall, F32),
        pltpu.VMEM(tall, F32),
        pltpu.VMEM((tiles, orows, cells), BF16),
        pltpu.VMEM(grid, F32),
        pltpu.VMEM(grid, F32),
        pltpu.VMEM(grid, F32),
        pltpu.VMEM((cells, cells), BF16),
        pltpu.VMEM((cells, cells), BF16),
        pltpu.VMEM((slots * lev, lev * rows), BF16),
        pltpu.VMEM((lev * rows, slots * lev), BF16),
        pltpu.VMEM((slots * lev, width), F32),
        pltpu.VMEM((slots * lev, touched), F32),
        pltpu.VMEM((slots, tiles * orows), BF16),
        pltpu.VMEM((tiles, orows), F32),
        pltpu.VMEM((tiles, orows), F32),
        pltpu.VMEM((slots * lev, touched), jnp.int32),
        pltpu.VMEM((slots * lev, touched), jnp.int32),
        pltpu.VMEM((slots * lev, touched), jnp.int32),
        pltpu.VMEM((slots * lev, touched), jnp.int32),
        pltpu.VMEM((2 * ITERS, slots * lev, touched), BF16),
        pltpu.VMEM((2 * ITERS, slots * lev, touched), BF16),
        pltpu.VMEM((ITERS, 2, 4 * lev, width), F32),
        pltpu.VMEM((ITERS, 2, 4 * lev, width), F32),
        pltpu.VMEM((ITERS, 3) + grid, F32),
        pltpu.VMEM((ITERS, 3) + grid, F32),
        dma((len(LOADS),)),
        dma((2, lev)),
        dma((1 + 2 * ITERS, n)),
        dma((1 + 2 * ITERS, n)),
        dma((ITERS, 2)),
        dma((ITERS, 2)),
        dma((ITERS, 3, lev)),
        dma((ITERS, 3, lev)),
    ]
    dual_model, obs_dual, increment = pl.pallas_call(
        functools.partial(kernel, n, cap),
        out_shape=(
            jax.ShapeDtypeStruct((1,) + grid, F32),
            jax.ShapeDtypeStruct((1, tiles, orows), F32),
            jax.ShapeDtypeStruct((1,) + grid, F32),
        ),
        in_specs=[hbm, hbm, vmem, hbm, hbm, hbm, hbm, smem, smem, vmem, hbm, vmem, vmem],
        out_specs=(hbm, vmem, hbm),
        scratch_shapes=scratch,
        compiler_params=pltpu.CompilerParams(
            collective_id=0, has_side_effects=True, vmem_limit_bytes=60 * 2**20
        ),
        name="assimilate",
    )(*args)
    results = (dual_model, increment, obs_dual)
    dual_model, increment, obs_dual = pl.pallas_call(
        deliver,
        out_shape=tuple(jax.ShapeDtypeStruct(r.shape, r.dtype) for r in results),
        in_specs=[hbm] * 3,
        out_specs=(hbm,) * 3,
        scratch_shapes=[dma((3, lev))],
        compiler_params=pltpu.CompilerParams(vmem_limit_bytes=60 * 2**20),
        name="deliver",
    )(*results)
    return (dual_model, obs_dual, increment)


def solution(mesh):
    in_specs = (
        P("tm", None, "space", None),
        P("tm", None, "space", None),
        P("tm", "space", None),
        P("tm", None, "space", None),
        P("tm", None, "space", None),
        P("tm", None, "space", None),
        P(None, "space", None),
        P(),
        P("tm", "space"),
        P("tm", "space", None),
        P("tm", "space", None, None),
        P("tm", "space", None),
        P("tm", "space", None),
    )
    out_specs = (P("tm", None, "space", None), P("tm", "space", None), P("tm", None, "space", None))
    return jax.shard_map(
        on_device, mesh=mesh, in_specs=in_specs, out_specs=out_specs, check_vma=False
    )
```

```python
import functools

import jax
import jax.numpy as jnp
from jax import lax
from jax.experimental import pallas as pl
from jax.experimental.pallas import tpu as pltpu
from jax.sharding import PartitionSpec as P

SUBSTEPS = 2
ITERS = 2
EDGE = 8
F32 = jnp.float32
BF16 = jnp.bfloat16
MESH = pl.DeviceIdType.MESH
LOADS = ("inc", "dual", "rhs", "err", "dec", "scale", "field", "jac")


def shift_of(size):
    assert size & (size - 1) == 0
    return size.bit_length() - 1


def lanes(block, index):
    return jnp.take_along_axis(block, index, axis=1, mode="promise_in_bounds")


def cells_to_levels(values, lev, touched):
    lane = lax.broadcasted_iota(jnp.int32, (values.shape[0], touched), 1)
    part = touched // lev
    found = []
    for l in range(lev):
        index = (lane & (part - 1)) * lev + l
        one = jnp.zeros((values.shape[0], touched), values.dtype)
        for b in range(lev):
            block = lanes(values[:, b * touched : (b + 1) * touched], index)
            one = jnp.where(lane >> shift_of(part) == b, block, one)
        found.append(one)
    return found


def levels_to_cells(values, lev, touched):
    lane = lax.broadcasted_iota(jnp.int32, values[0].shape, 1)
    part = touched // lev
    found = []
    for b in range(lev):
        index = b * part + (lane >> shift_of(lev))
        one = jnp.zeros(values[0].shape, values[0].dtype)
        for l in range(lev):
            one = jnp.where((lane & (lev - 1)) == l, lanes(values[l], index), one)
        found.append(one)
    return jnp.concatenate(found, axis=1)


def contract(a, b, dims):
    return lax.dot_general(a, b, (dims, ((), ())), preferred_element_type=F32)


def kernel(
    n, cap,
    inc_in, dual_in, dobs_in, rhs_in, err_in, dec_in, scale_in, diff_ref, owners_ref,
    cols_ref, jac_in, innov_ref, ovar_ref,
    dual_out, dobs_out, inc_out,
    inc, dual, rhs, err, dec, scale, field, jac,
    adj, mfield, source, pick, pick_t, lines, packed, vmat, image, obs_dual,
    req_s, req_r, col_lo, col_hi, msg_s, msg_r, halo_s, halo_r, pair_s, pair_r,
    load_sem, out_sem, a2a_send, a2a_recv, halo_send, halo_recv, pair_send, pair_recv,
):
    me = lax.axis_index("space")
    tm = lax.axis_index("tm")
    lev, rows, width = inc.shape
    tiles, touched = cols_ref.shape[1:]
    slots = n * cap
    span = cap * lev
    groups = width // 128
    own = pl.ds(EDGE, rows)

    def load(k, src, dst):
        return pltpu.make_async_copy(src, dst, load_sem.at[LOADS.index(k)])

    loads = {
        "inc": load("inc", inc_in.at[0], inc),
        "dual": load("dual", dual_in.at[0], dual),
        "rhs": load("rhs", rhs_in.at[0], rhs),
        "err": load("err", err_in.at[0], err),
        "dec": load("dec", dec_in.at[0], dec),
        "scale": load("scale", scale_in, scale.at[:, own]),
        "jac": load("jac", jac_in.at[0], jac),
    }
    field_0 = load("field", inc_in.at[0], field.at[:, own])
    field_1 = load("field", dual_in.at[0], field.at[:, own])

    @pl.when(tm == 0)
    def _():
        field_0.start()

    @pl.when(tm == 1)
    def _():
        field_1.start()

    for name in ("scale", "jac", "inc", "dual", "dec", "rhs", "err"):
        loads[name].start()

    barrier = pltpu.get_barrier_semaphore()

    def greet(k, c):
        pl.semaphore_signal(
            barrier, inc=1, device_id={"space": lax.rem(me + k, n)}, device_id_type=MESH
        )
        return c

    lax.fori_loop(1, n, greet, 0)
    pl.semaphore_signal(barrier, inc=1, device_id={"tm": 1 - tm}, device_id_type=MESH)

    zero_rows = jnp.zeros((EDGE, width), F32)
    for l in range(lev):
        for ref in (field, scale):
            ref[l, pl.ds(0, EDGE), :] = zero_rows
            ref[l, pl.ds(EDGE + rows, EDGE), :] = zero_rows

    owner = [owners_ref[0, t] for t in range(tiles)]
    slot_of = []
    for t in range(tiles):
        rank = jnp.int32(0)
        for u in range(t):
            rank = rank + jnp.where(owner[u] == owner[t], 1, 0)
        slot_of.append(owner[t] * cap + rank)
    slot_row = lax.broadcasted_iota(jnp.int32, (slots, touched), 0)
    wide_row = lax.broadcasted_iota(jnp.int32, (slots * lev, touched), 0) >> shift_of(lev)

    wanted = jnp.zeros((slots * lev, touched), jnp.int32)
    for t in range(tiles):
        wanted = jnp.where(wide_row == slot_of[t], cols_ref[0, pl.ds(t, 1), :], wanted)
    req_s[...] = wanted

    def block(i):
        return pl.ds(pl.multiple_of(i * span, span), span)

    def phase_refs(phase):
        if phase == 0:
            return req_s, req_r
        return msg_s.at[phase - 1], msg_r.at[phase - 1]

    def exchange(phase, to):
        src, dst = phase_refs(phase)
        return pltpu.make_async_remote_copy(
            src_ref=src.at[block(to)],
            dst_ref=dst.at[block(me)],
            send_sem=a2a_send.at[phase, to],
            recv_sem=a2a_recv.at[phase, me],
            device_id={"space": to},
            device_id_type=MESH,
        )

    def arrival(phase, frm):
        src, dst = phase_refs(phase)
        return pltpu.make_async_remote_copy(
            src_ref=src.at[block(frm)],
            dst_ref=dst.at[block(frm)],
            send_sem=a2a_send.at[phase, frm],
            recv_sem=a2a_recv.at[phase, frm],
            device_id={"space": frm},
            device_id_type=MESH,
        )

    def over_peers(act):
        def step(k, c):
            act(lax.rem(me + k, n))
            return c

        lax.fori_loop(1, n, step, 0)

    def send_all(phase):
        over_peers(lambda to: exchange(phase, to).start())
        src, dst = phase_refs(phase)
        dst[block(me), :] = src[block(me), :]

    def recv_all(phase):
        over_peers(lambda frm: arrival(phase, frm).wait_recv())

    pl.semaphore_wait(barrier, n)
    send_all(0)

    def halo_copy(it, way):
        count = 4 * lev if it == 0 else 2 * lev
        part = pl.ds(0, count)
        return pltpu.make_async_remote_copy(
            src_ref=halo_s.at[it, way, part],
            dst_ref=halo_r.at[it, way, part],
            send_sem=halo_send.at[it, way],
            recv_sem=halo_recv.at[it, way],
            device_id={"space": lax.rem(me + (n - 1 if way == 0 else 1), n)},
            device_id_type=MESH,
        )

    def halo_out(it):
        for way, first in ((0, EDGE), (1, EDGE + rows - 2)):
            for l in range(lev):
                halo_s[it, way, pl.ds(2 * l, 2), :] = field[l, pl.ds(first, 2), :]
                if it == 0:
                    halo_s[it, way, pl.ds(2 * (lev + l), 2), :] = scale[l, pl.ds(first, 2), :]

        @pl.when(me > 0)
        def _():
            halo_copy(it, 0).start()

        @pl.when(me < n - 1)
        def _():
            halo_copy(it, 1).start()

    def halo_in(it):
        def place(way, first):
            halo_copy(it, way).wait_recv()
            for l in range(lev):
                field[l, pl.ds(first, 2), :] = halo_r[it, way, pl.ds(2 * l, 2), :]
                if it == 0:
                    scale[l, pl.ds(first, 2), :] = halo_r[it, way, pl.ds(2 * (lev + l), 2), :]

        @pl.when(me < n - 1)
        def _():
            place(0, EDGE + rows)

        @pl.when(me > 0)
        def _():
            place(1, EDGE - 2)

    def pair_copy(it, kind, l):
        return pltpu.make_async_remote_copy(
            src_ref=pair_s.at[it, kind, l],
            dst_ref=pair_r.at[it, kind, l],
            send_sem=pair_send.at[it, kind, l],
            recv_sem=pair_recv.at[it, kind, l],
            device_id={"tm": 1 - tm},
            device_id_type=MESH,
        )

    def per_level(act):
        def step(l, c):
            act(l)
            return c

        lax.fori_loop(0, lev, step, 0)

    def model(l):
        factor = scale[l]
        current = field[l]
        tall = current.shape[0]
        for repeat in range(SUBSTEPS):
            scaled = factor * current
            laplace = (
                pltpu.roll(scaled, 1, 0)
                + pltpu.roll(scaled, tall - 1, 0)
                + pltpu.roll(scaled, 1, 1)
                + pltpu.roll(scaled, width - 1, 1)
                - 4.0 * scaled
            )
            current = factor * (scaled + diff_ref[l] * laplace)
        return current[EDGE : EDGE + rows]

    def adjoint_out(phase):
        rounded = obs_dual[...].astype(BF16).astype(F32)
        for t in range(tiles):
            row = jnp.where(slot_row == slot_of[t], rounded[t : t + 1, :], 0.0)
            vmat[:, pl.ds(t * touched, touched)] = row.astype(BF16)
        flat = jac[...].reshape(tiles * jac.shape[1], jac.shape[2])
        grad = contract(vmat[...], flat, ((1,), (0,)))
        for l, part in enumerate(cells_to_levels(grad, lev, touched)):
            packed[pl.ds(l, slots, stride=lev), :] = part
        phase_refs(phase)[0][...] = packed[...].astype(BF16)
        send_all(phase)

    def columns_out(phase):
        flat = inc[...].reshape(lev * rows, width).astype(BF16)
        lines[...] = contract(pick[...], flat, ((1,), (0,)))
        found = jnp.zeros((slots * lev, touched), F32)
        for h in range(groups):
            part = lanes(lines[:, h * 128 : (h + 1) * 128], col_lo[...])
            found = jnp.where(col_hi[...] == h, part, found)
        phase_refs(phase)[0][...] = found.astype(BF16)
        send_all(phase)

    def observe(phase):
        recv_all(phase)
        packed[...] = phase_refs(phase)[1][...].astype(F32)
        by_level = [packed[pl.ds(l, slots, stride=lev), :] for l in range(lev)]
        cells = levels_to_cells(by_level, lev, touched).astype(BF16)
        flat = jac[...].reshape(tiles * jac.shape[1], jac.shape[2])
        seen = contract(cells, flat, ((1,), (1,)))
        for t in range(tiles):
            mine = jnp.where(slot_row == slot_of[t], seen[:, t * touched : (t + 1) * touched], 0.0)
            image[pl.ds(t, 1), :] = jnp.sum(mine, axis=0, keepdims=True)
        variance = ovar_ref[0].astype(F32)
        held = obs_dual[...]
        residual = innov_ref[0].astype(F32) - variance * held - image[...]
        obs_dual[...] = held + residual / variance

    def spread(phase):
        recv_all(phase)
        packed[...] = phase_refs(phase)[1][...].astype(F32)
        lane_row = lax.broadcasted_iota(jnp.int32, (128, touched), 0)

        def slot_lines(s, c):
            here = pl.ds(pl.multiple_of(s * lev, lev), lev)
            values, high, low = packed[here, :], col_hi[here, :], col_lo[here, :]
            left = jnp.concatenate(
                [jnp.where(high == h, values, 0.0) for h in range(groups)], axis=0
            ).astype(BF16)
            places = jnp.concatenate([low] * (128 // lev), axis=0)
            onehot = jnp.where(places == lane_row, 1.0, 0.0).astype(BF16)
            line = contract(left, onehot, ((1,), (1,)))
            for h in range(groups):
                lines[here, pl.ds(h * 128, 128)] = line[h * lev : (h + 1) * lev]
            return c

        def several(s, c):
            for u in range(16):
                slot_lines(16 * s + u, c)
            return c

        lax.fori_loop(0, slots // 16, several, 0)
        whole = lines[...]
        high = whole.astype(BF16)
        low = (whole - high.astype(F32)).astype(BF16)
        total = contract(pick_t[...], high, ((1,), (0,))) + contract(
            pick_t[...], low, ((1,), (0,))
        )
        adj[...] = total.reshape(lev, rows, width)

    loads["scale"].wait()
    field_0.wait()
    halo_out(0)

    obs_dual[...] = dobs_in[0].astype(F32)
    loads["jac"].wait()
    adjoint_out(1)

    recv_all(0)
    cell = req_r[...]
    col_lo[...] = cell & 127
    col_hi[...] = (cell & (width - 1)) >> 7
    line_of = cell >> shift_of(width)
    level_of = lax.broadcasted_iota(jnp.int32, (slots * lev, touched), 0) & (lev - 1)
    place = level_of * rows + line_of
    lane = lax.broadcasted_iota(jnp.int32, (slots * lev, touched), 1)
    chosen = jnp.concatenate(
        [
            jnp.where(place == lane + first_lane, 1.0, 0.0)
            for first_lane in range(0, lev * rows, touched)
        ],
        axis=1,
    )
    pick[...] = chosen.astype(BF16)
    pick_t[...] = chosen.T.astype(BF16)

    loads["inc"].wait()
    columns_out(2)
    loads["dual"].wait()
    loads["dec"].wait()
    loads["rhs"].wait()
    loads["err"].wait()

    def forward_model(it):
        halo_in(it)

        def go(l):
            pair_s[it, 0, l] = model(l)
            pair_copy(it, 0, l).start()

        per_level(go)

    def backward_model(it):
        halo_in(it)

        def go(l):
            mfield[l] = model(l)

        per_level(go)

    def write_out(l, which):
        held, out = ((dual, dual_out), (inc, inc_out))[which]
        return pltpu.make_async_copy(held.at[l], out.at[0, l], out_sem.at[which, l])

    for it in range(ITERS):
        last = it == ITERS - 1
        grad_phase, cols_phase = 1 + 2 * it, 2 + 2 * it
        if it == 0:

            @pl.when(tm == 0)
            def _():
                forward_model(it)

            @pl.when(tm == 1)
            def _():
                backward_model(it)

        spread(grad_phase)

        @pl.when(tm == 1)
        def _():
            def go(l):
                upward = -dual[l] - adj[l]
                pair_s[it, 2, l] = mfield[l] + dec[l] * upward
                pair_copy(it, 2, l).start()
                r_model = rhs[l] - err[l] * dual[l] - inc[l]
                source[l] = r_model - err[l] * upward
                raised = dual[l] + upward
                dual[l] = raised
                if not last:
                    field[l, own, :] = raised
                else:
                    write_out(l, 0).start()

            per_level(go)
            if not last:
                halo_out(it + 1)

        if not last:
            observe(cols_phase)
            adjoint_out(grad_phase + 2)

        @pl.when(tm == 0)
        def _():
            if it > 0:
                forward_model(it)

            def go(l):
                pair_copy(it, 2, l).wait_recv()
                upward = pair_r[it, 2, l] - dual[l] - adj[l]
                along = rhs[l] - err[l] * dual[l] - inc[l] - err[l] * upward
                pair_s[it, 1, l] = along
                pair_copy(it, 1, l).start()
                dual[l] = dual[l] + upward
                moved = inc[l] + along
                inc[l] = moved
                if not last:
                    field[l, own, :] = moved
                else:
                    write_out(l, 0).start()
                    write_out(l, 1).start()

            per_level(go)
            if not last:
                halo_out(it + 1)

        if last:
            observe(cols_phase)
            dobs_out[0] = obs_dual[...]

        @pl.when(tm == 1)
        def _():
            if not last:
                backward_model(it + 1)

            def go(l):
                pair_copy(it, 0, l).wait_recv()
                pair_copy(it, 1, l).wait_recv()
                along = source[l] + pair_r[it, 0, l] + dec[l] * pair_r[it, 1, l]
                inc[l] = inc[l] + along
                if last:
                    write_out(l, 1).start()

            per_level(go)

        if not last:
            columns_out(cols_phase + 2)

    for phase in range(1 + 2 * ITERS):
        over_peers(lambda to: exchange(phase, to).wait_send())
    for it in range(ITERS):

        @pl.when(me > 0)
        def _():
            halo_copy(it, 0).wait_send()

        @pl.when(me < n - 1)
        def _():
            halo_copy(it, 1).wait_send()

        @pl.when(tm == 0)
        def _():
            per_level(lambda l: pair_copy(it, 0, l).wait_send())
            per_level(lambda l: pair_copy(it, 1, l).wait_send())

        @pl.when(tm == 1)
        def _():
            per_level(lambda l: pair_copy(it, 2, l).wait_send())

    per_level(lambda l: write_out(l, 0).wait())
    per_level(lambda l: write_out(l, 1).wait())


def deliver(*refs):
    count = (len(refs) - 2) // 3
    sources, targets, held = (refs[i * count : (i + 1) * count] for i in range(3))
    in_sem, out_sem = refs[-2:]
    parts = in_sem.shape[1]
    steps = []
    for k, (src, dst, mid) in enumerate(zip(sources, targets, held)):
        cuts = parts if len(src.shape) == 4 else 1
        size = src.shape[1] // cuts
        for part in range(cuts):
            here = pl.ds(part * size, size)
            steps.append(
                (
                    pltpu.make_async_copy(src.at[0, here], mid.at[here], in_sem.at[k, part]),
                    pltpu.make_async_copy(mid.at[here], dst.at[0, here], out_sem.at[k, part]),
                )
            )
    for read, write in steps:
        read.start()
    for read, write in steps:
        read.wait()
        write.start()
    for read, write in steps:
        write.wait()


def on_device(*args):
    increment_start, jacobian, tile_cols = args[0], args[10], args[9]
    lev, rows, width = increment_start.shape[1:]
    tiles, touched = tile_cols.shape[1:]
    orows = jacobian.shape[2]
    n = lax.axis_size("space")
    cap = max(2, 2 * tiles // n)
    slots = n * cap
    cells = touched * lev
    grid = (lev, rows, width)
    tall = (lev, rows + 2 * EDGE, width)
    hbm = pl.BlockSpec(memory_space=pl.ANY)
    vmem = pl.BlockSpec(memory_space=pltpu.VMEM)
    smem = pl.BlockSpec(memory_space=pltpu.SMEM)
    dma = pltpu.SemaphoreType.DMA
    scratch = [
        pltpu.VMEM(grid, F32),
        pltpu.VMEM(grid, F32),
        pltpu.VMEM(grid, F32),
        pltpu.VMEM(grid, F32),
        pltpu.VMEM(grid, F32),
        pltpu.VMEM(tall, F32),
        pltpu.VMEM(tall, F32),
        pltpu.VMEM((tiles, orows, cells), BF16),
        pltpu.VMEM(grid, F32),
        pltpu.VMEM(grid, F32),
        pltpu.VMEM(grid, F32),
        pltpu.VMEM((slots * lev, lev * rows), BF16),
        pltpu.VMEM((lev * rows, slots * lev), BF16),
        pltpu.VMEM((slots * lev, width), F32),
        pltpu.VMEM((slots * lev, touched), F32),
        pltpu.VMEM((slots, tiles * orows), BF16),
        pltpu.VMEM((tiles, orows), F32),
        pltpu.VMEM((tiles, orows), F32),
        pltpu.VMEM((slots * lev, touched), jnp.int32),
        pltpu.VMEM((slots * lev, touched), jnp.int32),
        pltpu.VMEM((slots * lev, touched), jnp.int32),
        pltpu.VMEM((slots * lev, touched), jnp.int32),
        pltpu.VMEM((2 * ITERS, slots * lev, touched), BF16),
        pltpu.VMEM((2 * ITERS, slots * lev, touched), BF16),
        pltpu.VMEM((ITERS, 2, 4 * lev, width), F32),
        pltpu.VMEM((ITERS, 2, 4 * lev, width), F32),
        pltpu.VMEM((ITERS, 3) + grid, F32),
        pltpu.VMEM((ITERS, 3) + grid, F32),
        dma((len(LOADS),)),
        dma((2, lev)),
        dma((1 + 2 * ITERS, n)),
        dma((1 + 2 * ITERS, n)),
        dma((ITERS, 2)),
        dma((ITERS, 2)),
        dma((ITERS, 3, lev)),
        dma((ITERS, 3, lev)),
    ]
    dual_model, obs_dual, increment = pl.pallas_call(
        functools.partial(kernel, n, cap),
        out_shape=(
            jax.ShapeDtypeStruct((1,) + grid, F32),
            jax.ShapeDtypeStruct((1, tiles, orows), F32),
            jax.ShapeDtypeStruct((1,) + grid, F32),
        ),
        in_specs=[hbm, hbm, vmem, hbm, hbm, hbm, hbm, smem, smem, vmem, hbm, vmem, vmem],
        out_specs=(hbm, vmem, hbm),
        scratch_shapes=scratch,
        compiler_params=pltpu.CompilerParams(
            collective_id=0, has_side_effects=True, vmem_limit_bytes=60 * 2**20
        ),
        name="assimilate",
    )(*args)
    results = (dual_model, increment, obs_dual)
    dual_model, increment, obs_dual = pl.pallas_call(
        deliver,
        out_shape=tuple(jax.ShapeDtypeStruct(r.shape, r.dtype) for r in results),
        in_specs=[hbm] * 3,
        out_specs=(hbm,) * 3,
        scratch_shapes=[pltpu.VMEM(r.shape[1:], r.dtype) for r in results] + [dma((3, 4))] * 2,
        compiler_params=pltpu.CompilerParams(vmem_limit_bytes=60 * 2**20),
        name="deliver",
    )(*results)
    return (dual_model, obs_dual, increment)


def solution(mesh):
    in_specs = (
        P("tm", None, "space", None),
        P("tm", None, "space", None),
        P("tm", "space", None),
        P("tm", None, "space", None),
        P("tm", None, "space", None),
        P("tm", None, "space", None),
        P(None, "space", None),
        P(),
        P("tm", "space"),
        P("tm", "space", None),
        P("tm", "space", None, None),
        P("tm", "space", None),
        P("tm", "space", None),
    )
    out_specs = (P("tm", None, "space", None), P("tm", "space", None), P("tm", None, "space", None))
    return jax.shard_map(
        on_device, mesh=mesh, in_specs=in_specs, out_specs=out_specs, check_vma=False
    )
```

```python
import functools

import jax
import jax.numpy as jnp
from jax import lax
from jax.experimental import pallas as pl
from jax.experimental.pallas import tpu as pltpu
from jax.sharding import PartitionSpec as P

SUBSTEPS = 2
ITERS = 2
EDGE = 8
F32 = jnp.float32
BF16 = jnp.bfloat16
MESH = pl.DeviceIdType.MESH
LOADS = ("inc", "dual", "rhs", "err", "dec", "scale", "field", "jac")


def shift_of(size):
    assert size & (size - 1) == 0
    return size.bit_length() - 1


def lanes(block, index):
    return jnp.take_along_axis(block, index, axis=1, mode="promise_in_bounds")


def cells_to_levels(values, lev, touched):
    lane = lax.broadcasted_iota(jnp.int32, (values.shape[0], touched), 1)
    part = touched // lev
    found = []
    for l in range(lev):
        index = (lane & (part - 1)) * lev + l
        one = jnp.zeros((values.shape[0], touched), values.dtype)
        for b in range(lev):
            block = lanes(values[:, b * touched : (b + 1) * touched], index)
            one = jnp.where(lane >> shift_of(part) == b, block, one)
        found.append(one)
    return found


def levels_to_cells(values, lev, touched):
    lane = lax.broadcasted_iota(jnp.int32, values[0].shape, 1)
    part = touched // lev
    found = []
    for b in range(lev):
        index = b * part + (lane >> shift_of(lev))
        one = jnp.zeros(values[0].shape, values[0].dtype)
        for l in range(lev):
            one = jnp.where((lane & (lev - 1)) == l, lanes(values[l], index), one)
        found.append(one)
    return jnp.concatenate(found, axis=1)


def contract(a, b, dims):
    return lax.dot_general(a, b, (dims, ((), ())), preferred_element_type=F32)


def kernel(
    n, cap,
    inc_in, dual_in, dobs_in, rhs_in, err_in, dec_in, scale_in, diff_ref, owners_ref,
    cols_ref, jac_in, innov_ref, ovar_ref,
    dual_out, dobs_out, inc_out,
    inc, dual, rhs, err, dec, scale, field, jac,
    adj, mfield, source, pick, pick_t, lines, packed, vmat, image, obs_dual,
    req_s, req_r, col_lo, col_hi, msg_s, msg_r, halo_s, halo_r, pair_s, pair_r,
    load_sem, out_sem, a2a_send, a2a_recv, halo_send, halo_recv, pair_send, pair_recv,
):
    me = lax.axis_index("space")
    tm = lax.axis_index("tm")
    lev, rows, width = inc.shape
    tiles, touched = cols_ref.shape[1:]
    slots = n * cap
    span = cap * lev
    groups = width // 128
    own = pl.ds(EDGE, rows)

    def load(k, src, dst):
        return pltpu.make_async_copy(src, dst, load_sem.at[LOADS.index(k)])

    loads = {
        "inc": load("inc", inc_in.at[0], inc),
        "dual": load("dual", dual_in.at[0], dual),
        "rhs": load("rhs", rhs_in.at[0], rhs),
        "err": load("err", err_in.at[0], err),
        "dec": load("dec", dec_in.at[0], dec),
        "scale": load("scale", scale_in, scale.at[:, own]),
        "jac": load("jac", jac_in.at[0], jac),
    }
    field_0 = load("field", inc_in.at[0], field.at[:, own])
    field_1 = load("field", dual_in.at[0], field.at[:, own])

    @pl.when(tm == 0)
    def _():
        field_0.start()

    @pl.when(tm == 1)
    def _():
        field_1.start()

    for name in ("scale", "jac", "inc", "dual", "dec", "rhs", "err"):
        loads[name].start()

    barrier = pltpu.get_barrier_semaphore()

    def greet(k, c):
        pl.semaphore_signal(
            barrier, inc=1, device_id={"space": lax.rem(me + k, n)}, device_id_type=MESH
        )
        return c

    lax.fori_loop(1, n, greet, 0)
    pl.semaphore_signal(barrier, inc=1, device_id={"tm": 1 - tm}, device_id_type=MESH)

    zero_rows = jnp.zeros((EDGE, width), F32)
    for l in range(lev):
        for ref in (field, scale):
            ref[l, pl.ds(0, EDGE), :] = zero_rows
            ref[l, pl.ds(EDGE + rows, EDGE), :] = zero_rows

    owner = [owners_ref[0, t] for t in range(tiles)]
    slot_of = []
    for t in range(tiles):
        rank = jnp.int32(0)
        for u in range(t):
            rank = rank + jnp.where(owner[u] == owner[t], 1, 0)
        slot_of.append(owner[t] * cap + rank)
    slot_row = lax.broadcasted_iota(jnp.int32, (slots, touched), 0)
    wide_row = lax.broadcasted_iota(jnp.int32, (slots * lev, touched), 0) >> shift_of(lev)

    wanted = jnp.zeros((slots * lev, touched), jnp.int32)
    for t in range(tiles):
        wanted = jnp.where(wide_row == slot_of[t], cols_ref[0, pl.ds(t, 1), :], wanted)
    req_s[...] = wanted

    def block(i):
        return pl.ds(pl.multiple_of(i * span, span), span)

    def phase_refs(phase):
        if phase == 0:
            return req_s, req_r
        return msg_s.at[phase - 1], msg_r.at[phase - 1]

    def exchange(phase, to):
        src, dst = phase_refs(phase)
        return pltpu.make_async_remote_copy(
            src_ref=src.at[block(to)],
            dst_ref=dst.at[block(me)],
            send_sem=a2a_send.at[phase, to],
            recv_sem=a2a_recv.at[phase, me],
            device_id={"space": to},
            device_id_type=MESH,
        )

    def arrival(phase, frm):
        src, dst = phase_refs(phase)
        return pltpu.make_async_remote_copy(
            src_ref=src.at[block(frm)],
            dst_ref=dst.at[block(frm)],
            send_sem=a2a_send.at[phase, frm],
            recv_sem=a2a_recv.at[phase, frm],
            device_id={"space": frm},
            device_id_type=MESH,
        )

    def over_peers(act):
        def step(k, c):
            act(lax.rem(me + k, n))
            return c

        lax.fori_loop(1, n, step, 0)

    def send_all(phase):
        over_peers(lambda to: exchange(phase, to).start())
        src, dst = phase_refs(phase)
        dst[block(me), :] = src[block(me), :]

    def recv_all(phase):
        over_peers(lambda frm: arrival(phase, frm).wait_recv())

    pl.semaphore_wait(barrier, n)
    send_all(0)

    def halo_copy(it, way):
        count = 4 * lev if it == 0 else 2 * lev
        part = pl.ds(0, count)
        return pltpu.make_async_remote_copy(
            src_ref=halo_s.at[it, way, part],
            dst_ref=halo_r.at[it, way, part],
            send_sem=halo_send.at[it, way],
            recv_sem=halo_recv.at[it, way],
            device_id={"space": lax.rem(me + (n - 1 if way == 0 else 1), n)},
            device_id_type=MESH,
        )

    def halo_out(it):
        for way, first in ((0, EDGE), (1, EDGE + rows - 2)):
            for l in range(lev):
                halo_s[it, way, pl.ds(2 * l, 2), :] = field[l, pl.ds(first, 2), :]
                if it == 0:
                    halo_s[it, way, pl.ds(2 * (lev + l), 2), :] = scale[l, pl.ds(first, 2), :]

        @pl.when(me > 0)
        def _():
            halo_copy(it, 0).start()

        @pl.when(me < n - 1)
        def _():
            halo_copy(it, 1).start()

    def halo_in(it):
        def place(way, first):
            halo_copy(it, way).wait_recv()
            for l in range(lev):
                field[l, pl.ds(first, 2), :] = halo_r[it, way, pl.ds(2 * l, 2), :]
                if it == 0:
                    scale[l, pl.ds(first, 2), :] = halo_r[it, way, pl.ds(2 * (lev + l), 2), :]

        @pl.when(me < n - 1)
        def _():
            place(0, EDGE + rows)

        @pl.when(me > 0)
        def _():
            place(1, EDGE - 2)

    def pair_copy(it, kind, l):
        return pltpu.make_async_remote_copy(
            src_ref=pair_s.at[it, kind, l],
            dst_ref=pair_r.at[it, kind, l],
            send_sem=pair_send.at[it, kind, l],
            recv_sem=pair_recv.at[it, kind, l],
            device_id={"tm": 1 - tm},
            device_id_type=MESH,
        )

    def per_level(act):
        def step(l, c):
            act(l)
            return c

        lax.fori_loop(0, lev, step, 0)

    def model(l):
        factor = scale[l]
        current = field[l]
        tall = current.shape[0]
        for repeat in range(SUBSTEPS):
            scaled = factor * current
            laplace = (
                pltpu.roll(scaled, 1, 0)
                + pltpu.roll(scaled, tall - 1, 0)
                + pltpu.roll(scaled, 1, 1)
                + pltpu.roll(scaled, width - 1, 1)
                - 4.0 * scaled
            )
            current = factor * (scaled + diff_ref[l] * laplace)
        return current[EDGE : EDGE + rows]

    def adjoint_out(phase):
        rounded = obs_dual[...].astype(BF16).astype(F32)
        for t in range(tiles):
            row = jnp.where(slot_row == slot_of[t], rounded[t : t + 1, :], 0.0)
            vmat[:, pl.ds(t * touched, touched)] = row.astype(BF16)
        flat = jac[...].reshape(tiles * jac.shape[1], jac.shape[2])
        grad = contract(vmat[...], flat, ((1,), (0,)))
        for l, part in enumerate(cells_to_levels(grad, lev, touched)):
            packed[pl.ds(l, slots, stride=lev), :] = part
        phase_refs(phase)[0][...] = packed[...].astype(BF16)
        send_all(phase)

    def columns_out(phase):
        flat = inc[...].reshape(lev * rows, width).astype(BF16)
        lines[...] = contract(pick[...], flat, ((1,), (0,)))
        found = jnp.zeros((slots * lev, touched), F32)
        for h in range(groups):
            part = lanes(lines[:, h * 128 : (h + 1) * 128], col_lo[...])
            found = jnp.where(col_hi[...] == h, part, found)
        phase_refs(phase)[0][...] = found.astype(BF16)
        send_all(phase)

    def observe(phase):
        recv_all(phase)
        packed[...] = phase_refs(phase)[1][...].astype(F32)
        by_level = [packed[pl.ds(l, slots, stride=lev), :] for l in range(lev)]
        cells = levels_to_cells(by_level, lev, touched).astype(BF16)
        flat = jac[...].reshape(tiles * jac.shape[1], jac.shape[2])
        seen = contract(flat, cells, ((1,), (1,)))
        for t in range(tiles):
            mine = jnp.where(slot_row == slot_of[t], seen[t * touched : (t + 1) * touched].T, 0.0)
            image[pl.ds(t, 1), :] = jnp.sum(mine, axis=0, keepdims=True)
        variance = ovar_ref[0].astype(F32)
        held = obs_dual[...]
        residual = innov_ref[0].astype(F32) - variance * held - image[...]
        obs_dual[...] = held + residual / variance

    def spread(phase):
        recv_all(phase)
        packed[...] = phase_refs(phase)[1][...].astype(F32)
        lane_row = lax.broadcasted_iota(jnp.int32, (128, touched), 0)

        def slot_lines(s, c):
            here = pl.ds(pl.multiple_of(s * lev, lev), lev)
            values, high, low = packed[here, :], col_hi[here, :], col_lo[here, :]
            left = jnp.concatenate(
                [jnp.where(high == h, values, 0.0) for h in range(groups)], axis=0
            ).astype(BF16)
            places = jnp.concatenate([low] * (128 // lev), axis=0)
            onehot = jnp.where(places == lane_row, 1.0, 0.0).astype(BF16)
            line = contract(left, onehot, ((1,), (1,)))
            for h in range(groups):
                lines[here, pl.ds(h * 128, 128)] = line[h * lev : (h + 1) * lev]
            return c

        def several(s, c):
            for u in range(16):
                slot_lines(16 * s + u, c)
            return c

        lax.fori_loop(0, slots // 16, several, 0)
        whole = lines[...]
        high = whole.astype(BF16)
        low = (whole - high.astype(F32)).astype(BF16)
        total = contract(pick_t[...], high, ((1,), (0,))) + contract(
            pick_t[...], low, ((1,), (0,))
        )
        adj[...] = total.reshape(lev, rows, width)

    loads["scale"].wait()
    field_0.wait()
    halo_out(0)

    obs_dual[...] = dobs_in[0].astype(F32)
    loads["jac"].wait()
    adjoint_out(1)

    recv_all(0)
    cell = req_r[...]
    col_lo[...] = cell & 127
    col_hi[...] = (cell & (width - 1)) >> 7
    line_of = cell >> shift_of(width)
    level_of = lax.broadcasted_iota(jnp.int32, (slots * lev, touched), 0) & (lev - 1)
    place = level_of * rows + line_of
    lane = lax.broadcasted_iota(jnp.int32, (slots * lev, touched), 1)
    chosen = jnp.concatenate(
        [
            jnp.where(place == lane + first_lane, 1.0, 0.0)
            for first_lane in range(0, lev * rows, touched)
        ],
        axis=1,
    )
    pick[...] = chosen.astype(BF16)
    pick_t[...] = chosen.T.astype(BF16)

    loads["inc"].wait()
    columns_out(2)
    loads["dual"].wait()
    loads["dec"].wait()
    loads["rhs"].wait()
    loads["err"].wait()

    def forward_model(it):
        halo_in(it)

        def go(l):
            pair_s[it, 0, l] = model(l)
            pair_copy(it, 0, l).start()

        per_level(go)

    def backward_model(it):
        halo_in(it)

        def go(l):
            mfield[l] = model(l)

        per_level(go)

    def write_out(l, which):
        held, out = ((dual, dual_out), (inc, inc_out))[which]
        return pltpu.make_async_copy(held.at[l], out.at[0, l], out_sem.at[which, l])

    for it in range(ITERS):
        last = it == ITERS - 1
        grad_phase, cols_phase = 1 + 2 * it, 2 + 2 * it
        if it == 0:

            @pl.when(tm == 0)
            def _():
                forward_model(it)

            @pl.when(tm == 1)
            def _():
                backward_model(it)

        spread(grad_phase)

        @pl.when(tm == 1)
        def _():
            def go(l):
                upward = -dual[l] - adj[l]
                pair_s[it, 2, l] = mfield[l] + dec[l] * upward
                pair_copy(it, 2, l).start()
                r_model = rhs[l] - err[l] * dual[l] - inc[l]
                source[l] = r_model - err[l] * upward
                raised = dual[l] + upward
                dual[l] = raised
                if not last:
                    field[l, own, :] = raised
                else:
                    write_out(l, 0).start()

            per_level(go)
            if not last:
                halo_out(it + 1)

        if not last:
            observe(cols_phase)
            adjoint_out(grad_phase + 2)

        @pl.when(tm == 0)
        def _():
            if it > 0:
                forward_model(it)

            def go(l):
                pair_copy(it, 2, l).wait_recv()
                upward = pair_r[it, 2, l] - dual[l] - adj[l]
                along = rhs[l] - err[l] * dual[l] - inc[l] - err[l] * upward
                pair_s[it, 1, l] = along
                pair_copy(it, 1, l).start()
                dual[l] = dual[l] + upward
                moved = inc[l] + along
                inc[l] = moved
                if not last:
                    field[l, own, :] = moved
                else:
                    write_out(l, 0).start()
                    write_out(l, 1).start()

            per_level(go)
            if not last:
                halo_out(it + 1)

        if last:
            observe(cols_phase)
            dobs_out[0] = obs_dual[...]

        @pl.when(tm == 1)
        def _():
            if not last:
                backward_model(it + 1)

            def go(l):
                pair_copy(it, 0, l).wait_recv()
                pair_copy(it, 1, l).wait_recv()
                along = source[l] + pair_r[it, 0, l] + dec[l] * pair_r[it, 1, l]
                inc[l] = inc[l] + along
                if last:
                    write_out(l, 1).start()

            per_level(go)

        if not last:
            columns_out(cols_phase + 2)

    for phase in range(1 + 2 * ITERS):
        over_peers(lambda to: exchange(phase, to).wait_send())
    for it in range(ITERS):

        @pl.when(me > 0)
        def _():
            halo_copy(it, 0).wait_send()

        @pl.when(me < n - 1)
        def _():
            halo_copy(it, 1).wait_send()

        @pl.when(tm == 0)
        def _():
            per_level(lambda l: pair_copy(it, 0, l).wait_send())
            per_level(lambda l: pair_copy(it, 1, l).wait_send())

        @pl.when(tm == 1)
        def _():
            per_level(lambda l: pair_copy(it, 2, l).wait_send())

    per_level(lambda l: write_out(l, 0).wait())
    per_level(lambda l: write_out(l, 1).wait())


def deliver(*refs):
    count = (len(refs) - 2) // 3
    sources, targets, held = (refs[i * count : (i + 1) * count] for i in range(3))
    in_sem, out_sem = refs[-2:]
    parts = in_sem.shape[1]
    steps = []
    for k, (src, dst, mid) in enumerate(zip(sources, targets, held)):
        cuts = parts if len(src.shape) == 4 else 1
        size = src.shape[1] // cuts
        for part in range(cuts):
            here = pl.ds(part * size, size)
            steps.append(
                (
                    pltpu.make_async_copy(src.at[0, here], mid.at[here], in_sem.at[k, part]),
                    pltpu.make_async_copy(mid.at[here], dst.at[0, here], out_sem.at[k, part]),
                )
            )
    for read, write in steps:
        read.start()
    for read, write in steps:
        read.wait()
        write.start()
    for read, write in steps:
        write.wait()


def on_device(*args):
    increment_start, jacobian, tile_cols = args[0], args[10], args[9]
    lev, rows, width = increment_start.shape[1:]
    tiles, touched = tile_cols.shape[1:]
    orows = jacobian.shape[2]
    n = lax.axis_size("space")
    cap = max(2, 2 * tiles // n)
    slots = n * cap
    cells = touched * lev
    grid = (lev, rows, width)
    tall = (lev, rows + 2 * EDGE, width)
    hbm = pl.BlockSpec(memory_space=pl.ANY)
    vmem = pl.BlockSpec(memory_space=pltpu.VMEM)
    smem = pl.BlockSpec(memory_space=pltpu.SMEM)
    dma = pltpu.SemaphoreType.DMA
    scratch = [
        pltpu.VMEM(grid, F32),
        pltpu.VMEM(grid, F32),
        pltpu.VMEM(grid, F32),
        pltpu.VMEM(grid, F32),
        pltpu.VMEM(grid, F32),
        pltpu.VMEM(tall, F32),
        pltpu.VMEM(tall, F32),
        pltpu.VMEM((tiles, orows, cells), BF16),
        pltpu.VMEM(grid, F32),
        pltpu.VMEM(grid, F32),
        pltpu.VMEM(grid, F32),
        pltpu.VMEM((slots * lev, lev * rows), BF16),
        pltpu.VMEM((lev * rows, slots * lev), BF16),
        pltpu.VMEM((slots * lev, width), F32),
        pltpu.VMEM((slots * lev, touched), F32),
        pltpu.VMEM((slots, tiles * orows), BF16),
        pltpu.VMEM((tiles, orows), F32),
        pltpu.VMEM((tiles, orows), F32),
        pltpu.VMEM((slots * lev, touched), jnp.int32),
        pltpu.VMEM((slots * lev, touched), jnp.int32),
        pltpu.VMEM((slots * lev, touched), jnp.int32),
        pltpu.VMEM((slots * lev, touched), jnp.int32),
        pltpu.VMEM((2 * ITERS, slots * lev, touched), BF16),
        pltpu.VMEM((2 * ITERS, slots * lev, touched), BF16),
        pltpu.VMEM((ITERS, 2, 4 * lev, width), F32),
        pltpu.VMEM((ITERS, 2, 4 * lev, width), F32),
        pltpu.VMEM((ITERS, 3) + grid, F32),
        pltpu.VMEM((ITERS, 3) + grid, F32),
        dma((len(LOADS),)),
        dma((2, lev)),
        dma((1 + 2 * ITERS, n)),
        dma((1 + 2 * ITERS, n)),
        dma((ITERS, 2)),
        dma((ITERS, 2)),
        dma((ITERS, 3, lev)),
        dma((ITERS, 3, lev)),
    ]
    dual_model, obs_dual, increment = pl.pallas_call(
        functools.partial(kernel, n, cap),
        out_shape=(
            jax.ShapeDtypeStruct((1,) + grid, F32),
            jax.ShapeDtypeStruct((1, tiles, orows), F32),
            jax.ShapeDtypeStruct((1,) + grid, F32),
        ),
        in_specs=[hbm, hbm, vmem, hbm, hbm, hbm, hbm, smem, smem, vmem, hbm, vmem, vmem],
        out_specs=(hbm, vmem, hbm),
        scratch_shapes=scratch,
        compiler_params=pltpu.CompilerParams(
            collective_id=0, has_side_effects=True, vmem_limit_bytes=60 * 2**20
        ),
        name="assimilate",
    )(*args)
    results = (dual_model, increment, obs_dual)
    dual_model, increment, obs_dual = pl.pallas_call(
        deliver,
        out_shape=tuple(jax.ShapeDtypeStruct(r.shape, r.dtype) for r in results),
        in_specs=[hbm] * 3,
        out_specs=(hbm,) * 3,
        scratch_shapes=[pltpu.VMEM(r.shape[1:], r.dtype) for r in results] + [dma((3, 4))] * 2,
        compiler_params=pltpu.CompilerParams(vmem_limit_bytes=60 * 2**20),
        name="deliver",
    )(*results)
    return (dual_model, obs_dual, increment)


def solution(mesh):
    in_specs = (
        P("tm", None, "space", None),
        P("tm", None, "space", None),
        P("tm", "space", None),
        P("tm", None, "space", None),
        P("tm", None, "space", None),
        P("tm", None, "space", None),
        P(None, "space", None),
        P(),
        P("tm", "space"),
        P("tm", "space", None),
        P("tm", "space", None, None),
        P("tm", "space", None),
        P("tm", "space", None),
    )
    out_specs = (P("tm", None, "space", None), P("tm", "space", None), P("tm", None, "space", None))
    return jax.shard_map(
        on_device, mesh=mesh, in_specs=in_specs, out_specs=out_specs, check_vma=False
    )
```
